32 devices in a mesh: seq: 8 (over z, y), ch: 4 (over x, core).
Axes of the slice: x: 2, y: 2, z: 4, core: 2. Of those that a mesh axis runs over, the one named last changes fastest.
Arguments:
- stream: bfloat16 [2048, 1536], P('seq', 'ch'), may hold values from -6 to 6
- norm_gain: float32 [9, 1536], replicated, may hold values from 0.25 to 1.75
- conv_weight: bfloat16 [8, 3, 1536, 768], P(None, None, 'seq', 'ch'), may hold values from -0.09375 to 0.09375
- conv_bias: float32 [8, 768], P(None, 'ch'), may hold values from -3 to 3
- point_weight: bfloat16 [8, 768, 1536], P(None, 'seq', 'ch'), may hold values from -0.21875 to 0.21875
- point_bias: float32 [8, 1536], P(None, 'ch'), may hold values from -2 to 2
- head_weight: bfloat16 [1536, 3840], P('seq', 'ch'), may hold values from -0.15625 to 0.15625
- head_bias: float32 [3840], P('ch'), may hold values from -3 to 3
- exon_start: int32 [512], replicated, may hold values from 0 to 2016, as said below
- exon_length: int32 [512], replicated, may hold values from 1 to 32
- exon_transcript: int32 [512], replicated, may hold values from 0 to 63, as said below
- transcript_slot: int32 [64], replicated, may hold values from 0 to 63, each once
Outputs:
- transcript_cov: float32 [64, 3840], P('seq', 'ch')
The draws below stay inside these ranges and needn't reach their ends.
Inputs may be any that keep to these rules, and one draw needn't show every extreme that they name: An exon of transcript t starts in bins t * 32 to t * 32 + 31, and exon_start[e] + exon_length[e] <= 2048. `exon_transcript`: never falls along the exons; every transcript has 1 to 15 exons, one exactly 15; transcripts 2 i and 2 i + 1 together have 2 * 8. `transcript_slot`: each row once.
All inputs are finite; a program needn't handle non-finite values.
Results may differ from the reference program's by a relative error of at most 0.00065.
Values may be sent and summed in bfloat16 or wider, within the bound.
A program may use at most 128 MiB of HBM per device.

```python
import jax
import jax.numpy as jnp
from jax import lax

CH = 1536
HID = 768
TRACKS = 3840
LAYERS = 8
EXONS_TX = 8
MOST_EXONS = 15
SPAN = 32
BINS = 2048
NTX = 64
NEXON = 512


def exon_owner(key):
    pairs = NTX // 2
    first = jax.random.randint(jax.random.fold_in(key, 11), (pairs,), 1, MOST_EXONS + 1).astype(jnp.int32)
    first = first.at[0].set(MOST_EXONS)
    per_tx = jnp.stack([first, 2 * EXONS_TX - first], axis=1).reshape(NTX)
    ends = jnp.cumsum(per_tx).astype(jnp.int32)
    exon_ids = jnp.arange(NEXON, dtype=jnp.int32)
    return jnp.sum((ends[None, :] <= exon_ids[:, None]).astype(jnp.int32), axis=1).astype(jnp.int32)


def draw_exon_transcript(key, part):
    return exon_owner(key)


def draw_exon_start(key, part):
    owner = exon_owner(key)
    offset = jax.random.randint(jax.random.fold_in(key, 12), (NEXON,), 0, SPAN).astype(jnp.int32)
    late = jax.random.randint(jax.random.fold_in(key, 13), (NEXON,), SPAN - 8, SPAN).astype(jnp.int32)
    next_owner = jnp.concatenate([owner[1:], jnp.full((1,), NTX, jnp.int32)])
    closing = next_owner != owner
    offset = jnp.where(closing, late, offset).astype(jnp.int32)
    start = jnp.minimum(owner * SPAN + offset, BINS - 32).astype(jnp.int32)
    start = start.at[0].set(0)
    start = start.at[NEXON - 1].set(BINS - 32)
    return start


def place_ends(entries, key, least, top_value):
    longest = entries.shape.index(max(entries.shape))
    spots = []
    for shift in (0, 1):
        where = [jax.random.randint(jax.random.fold_in(key, axis), (), 0, length) for axis, length in enumerate(entries.shape)]
        where[longest] = (where[longest] + shift) % entries.shape[longest]
        spots.append(tuple(where))
    return entries.at[spots[0]].set(least).at[spots[1]].set(top_value)


def shard_levels(own_key, extent, cuts, low, top_value):
    gain, own = 1.0, jax.random.fold_in(own_key, 6)
    for dim, blocks in cuts:
        draws = jnp.exp(jax.random.uniform(jax.random.fold_in(own, dim), (blocks,), jnp.float32, low / len(cuts), top_value / len(cuts)))
        gain = gain * jnp.repeat(draws, extent[dim] // blocks).reshape([-1 if axis == dim else 1 for axis in range(len(extent))])
    return gain


def bell_draw(key, shape, width, bound, split=(), kind=jnp.bfloat16):
    values = jax.random.normal(key, shape, jnp.float32) * width
    if len(split) > 0:
        values = shard_levels(key, shape, split, -0.22, 0.18) * values
    return jnp.clip(values, min=-bound, max=bound).astype(kind)


def setup_inputs(seed: int = 0) -> dict:
    key_of = jax.random.split(jax.random.key(seed), 13)
    stream = bell_draw(key_of[0], (BINS, CH), 1.0, 6.0, ((0, 8), (1, 4)))
    norm_gain = jnp.clip(1.0 + 0.15 * jax.random.normal(key_of[1], (LAYERS + 1, CH), jnp.float32), 0.25, 1.75)
    conv_weight = bell_draw(key_of[2], (LAYERS, 3, CH, HID), (3 * CH) ** -0.5, 0.09375, ((2, 8), (3, 4)))
    conv_bias = bell_draw(key_of[3], (LAYERS, HID), 0.5, 3.0, ((1, 4),), jnp.float32)
    point_weight = bell_draw(key_of[4], (LAYERS, HID, CH), HID ** -0.5, 0.21875, ((1, 8), (2, 4)))
    point_bias = bell_draw(key_of[5], (LAYERS, CH), 0.3, 2.0, ((1, 4),), jnp.float32)
    head_weight = bell_draw(key_of[6], (CH, TRACKS), CH ** -0.5, 0.15625, ((0, 8), (1, 4)))
    head_bias = bell_draw(key_of[7], (TRACKS,), 0.5, 3.0, ((0, 4),), jnp.float32)
    exon_start = draw_exon_start(jax.random.fold_in(key_of[12], 71), 0)
    exon_length = place_ends(jax.random.randint(key_of[9], (NEXON,), 1, 33), jax.random.fold_in(key_of[9], 1), 1, 32).astype(jnp.int32)
    exon_transcript = draw_exon_transcript(jax.random.fold_in(key_of[12], 71), 0)
    transcript_slot = jax.random.permutation(key_of[11], NTX).astype(jnp.int32)
    return dict(stream=stream, norm_gain=norm_gain, conv_weight=conv_weight, conv_bias=conv_bias, point_weight=point_weight, point_bias=point_bias, head_weight=head_weight, head_bias=head_bias, exon_start=exon_start, exon_length=exon_length, exon_transcript=exon_transcript, transcript_slot=transcript_slot)


def rms_scaled(values, gain_row):
    wide = values.astype(jnp.float32)
    scale = lax.rsqrt(lax.optimization_barrier(jnp.mean(wide * wide, axis=-1, keepdims=True)) + 1e-06)
    return wide * scale * gain_row

def reference(stream, norm_gain, conv_weight, conv_bias, point_weight, point_bias, head_weight, head_bias, exon_start, exon_length, exon_transcript, transcript_slot):
    resid = stream
    bin_count = stream.shape[0]
    for layer_idx in range(LAYERS):
        spread = 2 ** layer_idx
        act_rows = jax.nn.gelu(rms_scaled(resid, norm_gain[layer_idx]), approximate=False).astype(jnp.bfloat16)
        padded = jnp.pad(act_rows, ((spread, spread), (0, 0)))
        conv_sum = jnp.zeros((bin_count, conv_weight.shape[3]), jnp.float32)
        for tap_idx in range(3):
            conv_sum = conv_sum + jnp.dot(padded[tap_idx * spread:tap_idx * spread + bin_count], conv_weight[layer_idx, tap_idx], preferred_element_type=jnp.float32)
        hidden = jax.nn.gelu(conv_sum + conv_bias[layer_idx], approximate=False).astype(jnp.bfloat16)
        mixed = jnp.dot(hidden, point_weight[layer_idx], preferred_element_type=jnp.float32)
        resid = (resid.astype(jnp.float32) + mixed + point_bias[layer_idx]).astype(jnp.bfloat16)
    final_rows = rms_scaled(resid, norm_gain[LAYERS]).astype(jnp.bfloat16)
    coverage = jax.nn.softplus(jnp.dot(final_rows, head_weight, preferred_element_type=jnp.float32) + head_bias)
    bin_ids = jnp.arange(bin_count, dtype=jnp.int32)
    member = ((bin_ids[None, :] >= exon_start[:, None]) & (bin_ids[None, :] < (exon_start + exon_length)[:, None])).astype(jnp.bfloat16)
    owner_rows = transcript_slot[exon_transcript]
    select = (owner_rows[None, :] == jnp.arange(transcript_slot.shape[0], dtype=jnp.int32)[:, None]).astype(jnp.bfloat16)
    counts = jnp.dot(select, member, preferred_element_type=jnp.float32)
    total = jnp.dot(counts, coverage, precision=lax.Precision.HIGHEST)
    return jnp.log1p(total)
```

```python
import jax
import jax.numpy as jnp
from jax import lax
from jax.experimental import pallas as pl
from jax.experimental.pallas import tpu as pltpu
from jax.sharding import PartitionSpec as P

LAYERS = 8


def padded(block, sides, width):
    for axis, dim in sides:
        count = lax.axis_size(axis)
        forward = [(i, i + 1) for i in range(count - 1)]
        backward = [(target, source) for source, target in forward]
        low = lax.ppermute(
            lax.slice_in_dim(block, block.shape[dim] - width, None, axis=dim), axis, forward
        )
        high = lax.ppermute(lax.slice_in_dim(block, 0, width, axis=dim), axis, backward)
        block = jnp.concatenate([low, block, high], axis=dim)
    return block


def rms_scaled(values, gain_row):
    wide = values.astype(jnp.float32)
    scale = lax.rsqrt(jnp.mean(wide * wide, axis=-1, keepdims=True) + 1e-06)
    return wide * scale * gain_row


def local_plain(
    stream,
    norm_gain,
    conv_weight,
    conv_bias,
    point_weight,
    point_bias,
    head_weight,
    head_bias,
    exon_start,
    exon_length,
    exon_transcript,
    transcript_slot,
):
    bin_rows = stream.shape[0]
    resid = stream
    for layer_idx in range(LAYERS):
        spread = 2**layer_idx
        rimmed = padded(resid, (("seq", 0),), spread)
        full_rows = lax.all_gather(rimmed, "ch", axis=1, tiled=True)
        act_rows = jax.nn.gelu(
            rms_scaled(full_rows, norm_gain[layer_idx]), approximate=False
        ).astype(jnp.bfloat16)
        tap_rows = jnp.stack(
            [
                act_rows[0:bin_rows],
                act_rows[spread : spread + bin_rows],
                act_rows[2 * spread : 2 * spread + bin_rows],
            ]
        )
        conv_sum = jnp.einsum(
            "kbc,kch->bh",
            tap_rows,
            lax.all_gather(conv_weight[layer_idx], "seq", axis=1, tiled=True),
            preferred_element_type=jnp.float32,
        )
        hidden = jax.nn.gelu(conv_sum + conv_bias[layer_idx], approximate=False).astype(
            jnp.bfloat16
        )
        hidden_all = lax.all_gather(hidden, "ch", axis=1, tiled=True)
        mixed = jnp.dot(
            hidden_all,
            lax.all_gather(point_weight[layer_idx], "seq", axis=0, tiled=True),
            preferred_element_type=jnp.float32,
        )
        resid = (resid.astype(jnp.float32) + mixed + point_bias[layer_idx]).astype(jnp.bfloat16)
    final_all = lax.all_gather(resid, "ch", axis=1, tiled=True)
    final_rows = rms_scaled(final_all, norm_gain[LAYERS]).astype(jnp.bfloat16)
    logits = jnp.dot(
        final_rows,
        lax.all_gather(head_weight, "seq", axis=0, tiled=True),
        preferred_element_type=jnp.float32,
    )
    coverage = jax.nn.softplus(logits + head_bias)
    seq_index = lax.axis_index("seq")
    bin_ids = seq_index * bin_rows + jnp.arange(bin_rows, dtype=jnp.int32)
    member = (
        (bin_ids[None, :] >= exon_start[:, None])
        & (bin_ids[None, :] < (exon_start + exon_length)[:, None])
    ).astype(jnp.bfloat16)
    owner_rows = transcript_slot[exon_transcript]
    select = (
        owner_rows[None, :] == jnp.arange(transcript_slot.shape[0], dtype=jnp.int32)[:, None]
    ).astype(jnp.bfloat16)
    counts = jnp.dot(select, member, preferred_element_type=jnp.float32)
    total = lax.psum_scatter(
        jnp.dot(counts, coverage, precision=lax.Precision.HIGHEST),
        "seq",
        scatter_dimension=0,
        tiled=True,
    )
    return jnp.log1p(total)


SEQ = 8
CHS = 4
HALF = 96
MESH = pl.DeviceIdType.MESH


def gelu(values):
    return 0.5 * values * (1.0 + lax.erf(values * 0.7071067811865476))


def tower_kernel(
    w_ref,
    head_ref,
    x_ref,
    gain_ref,
    conv_bias_ref,
    point_bias_ref,
    head_bias_ref,
    counts_ref,
    out_ref,
    weights,
    heads,
    streams,
    act,
    low_ext,
    high_ext,
    middle,
    hid,
    point,
    partial,
    landed,
    local_sem,
    ring_send,
    ring_recv,
    x_send,
    x_recv,
    hid_send,
    hid_recv,
    halo_send,
    halo_recv,
    sum_send,
    sum_recv,
):
    seq = lax.axis_index("seq")
    ch = lax.axis_index("ch")
    rows = x_ref.shape[0]
    odd = seq % 2
    place = (1 - odd) * (seq // 2) + odd * (SEQ - 1 - seq // 2)

    def at_place(spot):
        spot = (spot + 2 * SEQ) % SEQ
        upper = spot // (SEQ // 2)
        return (1 - upper) * 2 * spot + upper * (2 * (SEQ - 1 - spot) + 1)

    ring_to = (at_place(place + 1), at_place(place - 1))
    sibling = ch + 1 - 2 * (ch % 2)
    across = (ch + 2) % CHS
    diagonal = (sibling + 2) % CHS

    barrier = pltpu.get_barrier_semaphore()
    for step in range(1, SEQ):
        pl.semaphore_signal(
            barrier, inc=1, device_id=((seq + step) % SEQ, ch), device_id_type=MESH
        )
    for peer in (sibling, across):
        pl.semaphore_signal(barrier, inc=1, device_id=(seq, peer), device_id_type=MESH)

    def own_copy(item):
        if item < LAYERS:
            return pltpu.make_async_copy(
                w_ref.at[item], weights.at[item, seq], local_sem.at[item]
            )
        return pltpu.make_async_copy(head_ref, heads.at[seq], local_sem.at[item])

    for item in range(LAYERS + 1):
        own_copy(item).start()
    streams[ch] = x_ref[...]
    pl.semaphore_wait(barrier, SEQ + 1)

    def reach(way, half):
        return 4 if way == half else 3

    def ring_copy(item, half, dist, way):
        origin = at_place(place - (dist - 1) if way == 0 else place + (dist - 1))
        part = pl.ds(half * HALF, HALF)
        if item < LAYERS:
            dst = weights.at[item, origin, part]
            src = w_ref.at[item, part] if dist == 1 else dst
        else:
            dst = heads.at[origin, part]
            src = head_ref.at[part] if dist == 1 else dst
        return pltpu.make_async_remote_copy(
            src_ref=src,
            dst_ref=dst,
            send_sem=ring_send.at[way, item, half, dist - 1],
            recv_sem=ring_recv.at[way, item, half, dist - 1],
            device_id=(ring_to[way], ch),
            device_id_type=MESH,
        )

    def service(item, half, dist):
        for way in (0, 1):
            far = reach(way, half)
            if dist <= far:
                ring_copy(item, half, dist, way).wait_recv()
                if dist < far:
                    ring_copy(item, half, dist + 1, way).start()
        if dist == 2 and item < LAYERS:
            for way in (0, 1):
                ring_copy(item + 1, half, 1, way).start()

    def slot(item, number):
        if item > LAYERS:
            return
        if number < 6:
            service(item, number % 2, number // 2 + 1)
        else:
            service(item, 0, 4)
            service(item, 1, 4)

    for half in (0, 1):
        for way in (0, 1):
            ring_copy(0, half, 1, way).start()

    def spread_copies(buffer, sends, recvs, turn):
        def copy(block, peer, number):
            return pltpu.make_async_remote_copy(
                src_ref=buffer.at[block],
                dst_ref=buffer.at[block],
                send_sem=sends.at[turn, number],
                recv_sem=recvs.at[turn, number],
                device_id=(seq, peer),
                device_id_type=MESH,
            )

        return copy(ch, across, 0), copy(ch, sibling, 1), copy(across, sibling, 2)

    def norm_rows(turn, first, count, finish):
        tile = 32

        @pl.loop(0, count // tile)
        def _(index):
            part = pl.ds(pl.multiple_of(first + index * tile, tile), tile)
            blocks = [streams[block, part, :].astype(jnp.float32) for block in range(CHS)]
            width = blocks[0].shape[1]
            squares = sum(jnp.sum(b * b, axis=1, keepdims=True) for b in blocks)
            scale = lax.rsqrt(squares / (width * CHS) + 1e-06)
            for block in range(CHS):
                lanes = pl.ds(block * width, width)
                normed = blocks[block] * scale * gain_ref[pl.ds(turn, 1), lanes]
                act[part, lanes] = finish(normed).astype(jnp.bfloat16)

    def gather_stream(turn):
        first, second, third = spread_copies(streams, x_send, x_recv, turn)
        finish = gelu if turn < LAYERS else (lambda normed: normed)
        first.start()
        second.start()
        slot(turn, 3)
        first.wait_recv()
        third.start()
        slot(turn, 4)
        second.wait_recv()
        third.wait_recv()
        norm_rows(turn, 0, rows // 2, finish)
        slot(turn, 5)
        norm_rows(turn, rows // 2, rows // 2, finish)
        for copy in (first, second, third):
            copy.wait_send()
        slot(turn, 6)
        own_copy(turn).wait()

    for number in (0, 1, 2):
        slot(0, number)

    for layer in range(LAYERS):
        spread = 2**layer
        rim = max(8, spread)
        pad = low_ext.shape[1] - rows
        gather_stream(layer)
        lows, highs = low_ext.at[layer % 2], high_ext.at[layer % 2]

        both = jnp.dot(
            act[...],
            weights[layer, :, :, 0:384].reshape(-1, 384),
            preferred_element_type=jnp.float32,
        )
        lows[pl.ds(pad, rows), :] = both[:, 0:256]
        middle[...] = both[:, 128:384]
        highs[pl.ds(0, rows), :] = jnp.dot(
            act[...],
            weights[layer, :, :, 384:640].reshape(-1, 256),
            preferred_element_type=jnp.float32,
        )

        up = pltpu.make_async_remote_copy(
            src_ref=lows.at[pl.ds(pad + rows - rim, rim)],
            dst_ref=lows.at[pl.ds(pad - rim, rim)],
            send_sem=halo_send.at[0, layer],
            recv_sem=halo_recv.at[0, layer],
            device_id=((seq + 1) % SEQ, ch),
            device_id_type=MESH,
        )
        down = pltpu.make_async_remote_copy(
            src_ref=highs.at[pl.ds(0, rim)],
            dst_ref=highs.at[pl.ds(rows, rim)],
            send_sem=halo_send.at[1, layer],
            recv_sem=halo_recv.at[1, layer],
            device_id=((seq + SEQ - 1) % SEQ, ch),
            device_id_type=MESH,
        )

        @pl.when(seq < SEQ - 1)
        def _():
            up.start()

        @pl.when(seq > 0)
        def _():
            down.start()

        slot(layer + 1, 0)

        for block in range(SEQ):
            here = pl.ds(block * HALF, HALF)
            point[here, 0:128] = weights[layer, block, 0:HALF, 640:768]
            point[here, 128:256] = weights[layer, block, HALF : 2 * HALF, 640:768]
            near = weights[layer, block, 0:HALF, 512:640].astype(jnp.float32)
            far = weights[layer, block, HALF : 2 * HALF, 512:640].astype(jnp.float32)
            lane = lax.broadcasted_iota(jnp.int32, near.shape, 1)
            point[here, 256:384] = jnp.where(
                lane < 64, pltpu.roll(near, 64, 1), far
            ).astype(jnp.bfloat16)

        @pl.when(seq > 0)
        def _():
            up.wait_recv()

        @pl.when(seq == 0)
        def _():
            lows[pl.ds(pad - rim, rim), :] = jnp.zeros((rim, 256), jnp.float32)

        @pl.when(seq < SEQ - 1)
        def _():
            down.wait_recv()

        @pl.when(seq == SEQ - 1)
        def _():
            highs[pl.ds(rows, rim), :] = jnp.zeros((rim, 256), jnp.float32)

        tile = 64
        for start in range(0, rows, tile):
            conv = (
                low_ext[layer % 2, pl.ds(pad - spread + start, tile), :]
                + pltpu.roll(middle[pl.ds(start, tile), :], 192, 1)
                + high_ext[layer % 2, pl.ds(spread + start, tile), :]
                + conv_bias_ref[pl.ds(layer, 1), :]
            )
            hid[ch, pl.ds(start, tile), :] = gelu(conv).astype(jnp.bfloat16)

        first, second, third = spread_copies(hid, hid_send, hid_recv, layer)
        first.start()
        second.start()

        @pl.when(seq < SEQ - 1)
        def _():
            up.wait_send()

        @pl.when(seq > 0)
        def _():
            down.wait_send()

        slot(layer + 1, 1)
        first.wait_recv()
        third.start()
        slot(layer + 1, 2)
        second.wait_recv()
        third.wait_recv()
        mixed = streams[ch].astype(jnp.float32) + point_bias_ref[pl.ds(layer, 1), :]
        total = None
        for block in range(CHS):
            term = jnp.dot(
                hid[block, :, 0:192],
                point[block * 192 : (block + 1) * 192, :],
                preferred_element_type=jnp.float32,
            )
            total = term if total is None else total + term
        streams[ch] = (mixed + total).astype(jnp.bfloat16)
        for copy in (first, second, third):
            copy.wait_send()

    gather_stream(LAYERS)

    for start in range(0, heads.shape[2], 256):
        lanes = pl.ds(start, 256)
        logits = (
            jnp.dot(
                act[...],
                heads[:, :, start : start + 256].reshape(-1, 256),
                preferred_element_type=jnp.float32,
            )
            + head_bias_ref[:, lanes]
        )
        cover = jnp.maximum(logits, 0.0) + jnp.log1p(jnp.exp(-jnp.abs(logits)))
        sums = None
        for _ in range(3):
            piece = cover.astype(jnp.bfloat16)
            term = jnp.dot(counts_ref[...], piece, preferred_element_type=jnp.float32)
            sums = term if sums is None else sums + term
            cover = cover - piece.astype(jnp.float32)
        partial[:, :, lanes] = sums.reshape(SEQ, -1, 256)

    def sum_copy(step):
        target = (seq + step) % SEQ
        return pltpu.make_async_remote_copy(
            src_ref=partial.at[target],
            dst_ref=landed.at[step - 1],
            send_sem=sum_send.at[step - 1],
            recv_sem=sum_recv.at[step - 1],
            device_id=(target, ch),
            device_id_type=MESH,
        )

    for step in range(1, SEQ):
        sum_copy(step).start()
    for item in range(LAYERS + 1):
        for half in (0, 1):
            for way in (0, 1):
                for dist in range(1, reach(way, half) + 1):
                    ring_copy(item, half, dist, way).wait_send()
    result = partial[seq]
    for step in range(1, SEQ):
        sum_copy(step).wait_recv()
        result = result + landed[step - 1]
    out_ref[...] = jnp.log1p(result)[:, : out_ref.shape[1]]
    for step in range(1, SEQ):
        sum_copy(step).wait_send()


def exon_counts(bin_rows, exon_start, exon_length, exon_transcript, transcript_slot):
    bin_ids = lax.axis_index("seq") * bin_rows + jnp.arange(bin_rows, dtype=jnp.int32)
    member = (
        (bin_ids[None, :] >= exon_start[:, None])
        & (bin_ids[None, :] < (exon_start + exon_length)[:, None])
    ).astype(jnp.bfloat16)
    owner_rows = transcript_slot[exon_transcript]
    select = (
        owner_rows[None, :] == jnp.arange(transcript_slot.shape[0], dtype=jnp.int32)[:, None]
    ).astype(jnp.bfloat16)
    return jnp.dot(select, member, preferred_element_type=jnp.float32)


def local_kernel(
    stream,
    norm_gain,
    conv_weight,
    conv_bias,
    point_weight,
    point_bias,
    head_weight,
    head_bias,
    exon_start,
    exon_length,
    exon_transcript,
    transcript_slot,
):
    rows, width = stream.shape
    depth = conv_weight.shape[2]
    tracks = head_weight.shape[1]
    wide = -(-tracks // 256) * 256
    slots = transcript_slot.shape[0]
    counts = exon_counts(rows, exon_start, exon_length, exon_transcript, transcript_slot).astype(
        jnp.bfloat16
    )
    last = point_weight[:, :, 256:384]
    packed = jnp.concatenate(
        [
            conv_weight[:, 0],
            conv_weight[:, 1],
            conv_weight[:, 2],
            jnp.concatenate([last[:, :, 0:64], last[:, :, 64:128]], axis=1),
            jnp.concatenate([point_weight[:, :, 0:128], point_weight[:, :, 128:256]], axis=1),
        ],
        axis=2,
    )
    vmem = pl.BlockSpec(memory_space=pltpu.VMEM)
    dma = pltpu.SemaphoreType.DMA
    return pl.pallas_call(
        tower_kernel,
        out_shape=jax.ShapeDtypeStruct((slots // SEQ, tracks), jnp.float32),
        in_specs=[vmem] * 8,
        out_specs=vmem,
        scratch_shapes=[
            pltpu.VMEM((LAYERS, SEQ, depth, 768), jnp.bfloat16),
            pltpu.VMEM((SEQ, depth, wide), jnp.bfloat16),
            pltpu.VMEM((CHS, rows, width), jnp.bfloat16),
            pltpu.VMEM((rows, CHS * width), jnp.bfloat16),
            pltpu.VMEM((2, rows + 128, 256), jnp.float32),
            pltpu.VMEM((2, rows + 128, 256), jnp.float32),
            pltpu.VMEM((rows, 256), jnp.float32),
            pltpu.VMEM((CHS, rows, 256), jnp.bfloat16),
            pltpu.VMEM((SEQ * HALF, width), jnp.bfloat16),
            pltpu.VMEM((SEQ, slots // SEQ, wide), jnp.float32),
            pltpu.VMEM((SEQ - 1, slots // SEQ, wide), jnp.float32),
            dma((LAYERS + 1,)),
            dma((2, LAYERS + 1, 2, 4)),
            dma((2, LAYERS + 1, 2, 4)),
            dma((LAYERS + 1, 3)),
            dma((LAYERS + 1, 3)),
            dma((LAYERS, 3)),
            dma((LAYERS, 3)),
            dma((2, LAYERS)),
            dma((2, LAYERS)),
            dma((SEQ - 1,)),
            dma((SEQ - 1,)),
        ],
        compiler_params=pltpu.CompilerParams(
            collective_id=0, has_side_effects=True, vmem_limit_bytes=56 * 2**20
        ),
        cost_estimate=pl.CostEstimate(
            flops=6_000_000_000, bytes_accessed=4_000_000, transcendentals=4_000_000
        ),
    )(
        packed,
        jnp.pad(head_weight, ((0, 0), (0, wide - tracks))),
        stream,
        norm_gain,
        jnp.pad(conv_bias, ((0, 0), (0, 256 - conv_bias.shape[1]))),
        point_bias,
        jnp.pad(head_bias, (0, wide - tracks))[None, :],
        counts,
    )


def local(*args):
    stream, conv_weight, point_weight = args[0], args[2], args[4]
    fits = (
        lax.axis_size("seq") == SEQ
        and lax.axis_size("ch") == CHS
        and stream.shape == (256, 384)
        and conv_weight.shape[2:] == (192, 192)
        and point_weight.shape[1:] == (HALF, 384)
        and args[11].shape[0] == 8 * SEQ
    )
    return local_kernel(*args) if fits else local_plain(*args)


def solution(mesh):
    placed = (
        P("seq", "ch"),
        P(),
        P(None, None, "seq", "ch"),
        P(None, "ch"),
        P(None, "seq", "ch"),
        P(None, "ch"),
        P("seq", "ch"),
        P("ch"),
        P(),
        P(),
        P(),
        P(),
    )
    return jax.shard_map(
        local, mesh=mesh, in_specs=placed, out_specs=P("seq", "ch"), check_vma=False
    )
```

```python
import jax
import jax.numpy as jnp
from jax import lax
from jax.experimental import pallas as pl
from jax.experimental.pallas import tpu as pltpu
from jax.sharding import PartitionSpec as P

LAYERS = 8


def padded(block, sides, width):
    for axis, dim in sides:
        count = lax.axis_size(axis)
        forward = [(i, i + 1) for i in range(count - 1)]
        backward = [(target, source) for source, target in forward]
        low = lax.ppermute(
            lax.slice_in_dim(block, block.shape[dim] - width, None, axis=dim), axis, forward
        )
        high = lax.ppermute(lax.slice_in_dim(block, 0, width, axis=dim), axis, backward)
        block = jnp.concatenate([low, block, high], axis=dim)
    return block


def rms_scaled(values, gain_row):
    wide = values.astype(jnp.float32)
    scale = lax.rsqrt(jnp.mean(wide * wide, axis=-1, keepdims=True) + 1e-06)
    return wide * scale * gain_row


def local_plain(
    stream,
    norm_gain,
    conv_weight,
    conv_bias,
    point_weight,
    point_bias,
    head_weight,
    head_bias,
    exon_start,
    exon_length,
    exon_transcript,
    transcript_slot,
):
    bin_rows = stream.shape[0]
    resid = stream
    for layer_idx in range(LAYERS):
        spread = 2**layer_idx
        rimmed = padded(resid, (("seq", 0),), spread)
        full_rows = lax.all_gather(rimmed, "ch", axis=1, tiled=True)
        act_rows = jax.nn.gelu(
            rms_scaled(full_rows, norm_gain[layer_idx]), approximate=False
        ).astype(jnp.bfloat16)
        tap_rows = jnp.stack(
            [
                act_rows[0:bin_rows],
                act_rows[spread : spread + bin_rows],
                act_rows[2 * spread : 2 * spread + bin_rows],
            ]
        )
        conv_sum = jnp.einsum(
            "kbc,kch->bh",
            tap_rows,
            lax.all_gather(conv_weight[layer_idx], "seq", axis=1, tiled=True),
            preferred_element_type=jnp.float32,
        )
        hidden = jax.nn.gelu(conv_sum + conv_bias[layer_idx], approximate=False).astype(
            jnp.bfloat16
        )
        hidden_all = lax.all_gather(hidden, "ch", axis=1, tiled=True)
        mixed = jnp.dot(
            hidden_all,
            lax.all_gather(point_weight[layer_idx], "seq", axis=0, tiled=True),
            preferred_element_type=jnp.float32,
        )
        resid = (resid.astype(jnp.float32) + mixed + point_bias[layer_idx]).astype(jnp.bfloat16)
    final_all = lax.all_gather(resid, "ch", axis=1, tiled=True)
    final_rows = rms_scaled(final_all, norm_gain[LAYERS]).astype(jnp.bfloat16)
    logits = jnp.dot(
        final_rows,
        lax.all_gather(head_weight, "seq", axis=0, tiled=True),
        preferred_element_type=jnp.float32,
    )
    coverage = jax.nn.softplus(logits + head_bias)
    seq_index = lax.axis_index("seq")
    bin_ids = seq_index * bin_rows + jnp.arange(bin_rows, dtype=jnp.int32)
    member = (
        (bin_ids[None, :] >= exon_start[:, None])
        & (bin_ids[None, :] < (exon_start + exon_length)[:, None])
    ).astype(jnp.bfloat16)
    owner_rows = transcript_slot[exon_transcript]
    select = (
        owner_rows[None, :] == jnp.arange(transcript_slot.shape[0], dtype=jnp.int32)[:, None]
    ).astype(jnp.bfloat16)
    counts = jnp.dot(select, member, preferred_element_type=jnp.float32)
    total = lax.psum_scatter(
        jnp.dot(counts, coverage, precision=lax.Precision.HIGHEST),
        "seq",
        scatter_dimension=0,
        tiled=True,
    )
    return jnp.log1p(total)


SEQ = 8
CHS = 4
HALF = 96
MESH = pl.DeviceIdType.MESH


def gelu(values):
    return 0.5 * values * (1.0 + lax.erf(values * 0.7071067811865476))


def tower_kernel(
    x_ref,
    gain_ref,
    conv_ref,
    conv_bias_ref,
    point_ref,
    point_bias_ref,
    head_ref,
    head_bias_ref,
    start_ref,
    length_ref,
    owner_ref,
    slot_ref,
    out_ref,
    weights,
    heads,
    streams,
    act,
    low_ext,
    high_ext,
    middle,
    hid,
    point,
    partial,
    landed,
    counts,
    conv_bias,
    head_bias,
    ring_send,
    ring_recv,
    x_send,
    x_recv,
    hid_send,
    hid_recv,
    halo_send,
    halo_recv,
    sum_send,
    sum_recv,
):
    seq = lax.axis_index("seq")
    ch = lax.axis_index("ch")
    rows = x_ref.shape[0]
    odd = seq % 2
    place = (1 - odd) * (seq // 2) + odd * (SEQ - 1 - seq // 2)

    def at_place(spot):
        spot = (spot + 2 * SEQ) % SEQ
        upper = spot // (SEQ // 2)
        return (1 - upper) * 2 * spot + upper * (2 * (SEQ - 1 - spot) + 1)

    ring_to = (at_place(place + 1), at_place(place - 1))
    sibling = ch + 1 - 2 * (ch % 2)
    across = (ch + 2) % CHS
    diagonal = (sibling + 2) % CHS

    barrier = pltpu.get_barrier_semaphore()
    for step in range(1, SEQ):
        pl.semaphore_signal(
            barrier, inc=1, device_id=((seq + step) % SEQ, ch), device_id_type=MESH
        )
    for peer in (sibling, across):
        pl.semaphore_signal(barrier, inc=1, device_id=(seq, peer), device_id_type=MESH)

    def pack(item):
        if item < LAYERS:
            last = point_ref[item, :, 256:384]
            strip = jnp.concatenate([last[:, 0:64], last[:, 64:128]], axis=0)
            own = weights.at[item, seq]
            own[:, 0:640] = jnp.concatenate(
                [conv_ref[item, 0], conv_ref[item, 1], conv_ref[item, 2], strip], axis=1
            )
            own[0:HALF, 640:768] = point_ref[item, :, 0:128]
            own[HALF : 2 * HALF, 640:768] = point_ref[item, :, 128:256]
        else:
            depth, tracks = head_ref.shape
            tail = tracks // 128 * 128
            own = heads.at[seq]
            own[:, tail:] = jnp.zeros((depth, heads.shape[2] - tail), jnp.bfloat16)
            own[:, 0:tracks] = head_ref[...]

    pack(0)
    streams[ch] = x_ref[...]
    pl.semaphore_wait(barrier, SEQ + 1)

    def reach(way, half):
        return 4 if way == half else 3

    def ring_copy(item, half, dist, way):
        origin = at_place(place - (dist - 1) if way == 0 else place + (dist - 1))
        part = pl.ds(half * HALF, HALF)
        if item < LAYERS:
            block = weights.at[item, origin, part]
        else:
            block = heads.at[origin, part]
        return pltpu.make_async_remote_copy(
            src_ref=block,
            dst_ref=block,
            send_sem=ring_send.at[way, item, half, dist - 1],
            recv_sem=ring_recv.at[way, item, half, dist - 1],
            device_id=(ring_to[way], ch),
            device_id_type=MESH,
        )

    def service(item, half, dist):
        for way in (0, 1):
            far = reach(way, half)
            if dist <= far:
                ring_copy(item, half, dist, way).wait_recv()
                if dist < far:
                    ring_copy(item, half, dist + 1, way).start()
        if dist == 2 and item < LAYERS:
            for way in (0, 1):
                ring_copy(item + 1, half, 1, way).start()

    def slot(item, number):
        if item > LAYERS:
            return
        if number < 6:
            service(item, number % 2, number // 2 + 1)
        else:
            service(item, 0, 4)
            service(item, 1, 4)

    for half in (0, 1):
        for way in (0, 1):
            ring_copy(0, half, 1, way).start()
    for item in range(1, LAYERS + 1):
        pack(item)

    slots = slot_ref.shape[1]
    bins = seq * rows + lax.broadcasted_iota(jnp.int32, (rows, start_ref.shape[1]), 0)
    member = (bins >= start_ref[...]) & (bins < start_ref[...] + length_ref[...])
    names = lax.broadcasted_iota(jnp.int32, (slots, owner_ref.shape[1]), 0)
    owned = lax.dot_general(
        jnp.where(names == owner_ref[...], 1.0, 0.0).astype(jnp.bfloat16),
        jnp.where(member, 1.0, 0.0).astype(jnp.bfloat16),
        (((1,), (1,)), ((), ())),
        preferred_element_type=jnp.float32,
    )
    order = lax.broadcasted_iota(jnp.int32, (slots, slots), 0) == slot_ref[...]
    counts[...] = jnp.dot(
        jnp.where(order, 1.0, 0.0).astype(jnp.bfloat16),
        owned.astype(jnp.bfloat16),
        preferred_element_type=jnp.float32,
    ).astype(jnp.bfloat16)
    conv_bias[...] = jnp.zeros_like(conv_bias)
    conv_bias[:, 0 : conv_bias_ref.shape[1]] = conv_bias_ref[...]
    head_bias[...] = jnp.zeros_like(head_bias)
    head_bias[:, 0 : head_bias_ref.shape[1]] = head_bias_ref[...]

    def spread_copies(buffer, sends, recvs, turn):
        def copy(block, peer, number):
            return pltpu.make_async_remote_copy(
                src_ref=buffer.at[block],
                dst_ref=buffer.at[block],
                send_sem=sends.at[turn, number],
                recv_sem=recvs.at[turn, number],
                device_id=(seq, peer),
                device_id_type=MESH,
            )

        return copy(ch, across, 0), copy(ch, sibling, 1), copy(across, sibling, 2)

    def norm_rows(turn, first, count, finish):
        tile = 32

        @pl.loop(0, count // tile)
        def _(index):
            part = pl.ds(pl.multiple_of(first + index * tile, tile), tile)
            blocks = [streams[block, part, :].astype(jnp.float32) for block in range(CHS)]
            width = blocks[0].shape[1]
            squares = sum(jnp.sum(b * b, axis=1, keepdims=True) for b in blocks)
            scale = lax.rsqrt(squares / (width * CHS) + 1e-06)
            for block in range(CHS):
                lanes = pl.ds(block * width, width)
                normed = blocks[block] * scale * gain_ref[pl.ds(turn, 1), lanes]
                act[part, lanes] = finish(normed).astype(jnp.bfloat16)

    def gather_stream(turn):
        first, second, third = spread_copies(streams, x_send, x_recv, turn)
        finish = gelu if turn < LAYERS else (lambda normed: normed)
        first.start()
        second.start()
        slot(turn, 3)
        first.wait_recv()
        third.start()
        slot(turn, 4)
        second.wait_recv()
        third.wait_recv()
        norm_rows(turn, 0, rows // 2, finish)
        slot(turn, 5)
        norm_rows(turn, rows // 2, rows // 2, finish)
        for copy in (first, second, third):
            copy.wait_send()
        slot(turn, 6)

    for number in (0, 1, 2):
        slot(0, number)

    for layer in range(LAYERS):
        spread = 2**layer
        rim = max(8, spread)
        pad = low_ext.shape[1] - rows
        gather_stream(layer)
        lows, highs = low_ext.at[layer % 2], high_ext.at[layer % 2]

        both = jnp.dot(
            act[...],
            weights[layer, :, :, 0:384].reshape(-1, 384),
            preferred_element_type=jnp.float32,
        )
        lows[pl.ds(pad, rows), :] = both[:, 0:256]
        middle[...] = both[:, 128:384]
        highs[pl.ds(0, rows), :] = jnp.dot(
            act[...],
            weights[layer, :, :, 384:640].reshape(-1, 256),
            preferred_element_type=jnp.float32,
        )

        up = pltpu.make_async_remote_copy(
            src_ref=lows.at[pl.ds(pad + rows - rim, rim)],
            dst_ref=lows.at[pl.ds(pad - rim, rim)],
            send_sem=halo_send.at[0, layer],
            recv_sem=halo_recv.at[0, layer],
            device_id=((seq + 1) % SEQ, ch),
            device_id_type=MESH,
        )
        down = pltpu.make_async_remote_copy(
            src_ref=highs.at[pl.ds(0, rim)],
            dst_ref=highs.at[pl.ds(rows, rim)],
            send_sem=halo_send.at[1, layer],
            recv_sem=halo_recv.at[1, layer],
            device_id=((seq + SEQ - 1) % SEQ, ch),
            device_id_type=MESH,
        )

        @pl.when(seq < SEQ - 1)
        def _():
            up.start()

        @pl.when(seq > 0)
        def _():
            down.start()

        slot(layer + 1, 0)

        for block in range(SEQ):
            here = pl.ds(block * HALF, HALF)
            point[here, 0:128] = weights[layer, block, 0:HALF, 640:768]
            point[here, 128:256] = weights[layer, block, HALF : 2 * HALF, 640:768]
            near = weights[layer, block, 0:HALF, 512:640].astype(jnp.float32)
            far = weights[layer, block, HALF : 2 * HALF, 512:640].astype(jnp.float32)
            lane = lax.broadcasted_iota(jnp.int32, near.shape, 1)
            point[here, 256:384] = jnp.where(
                lane < 64, pltpu.roll(near, 64, 1), far
            ).astype(jnp.bfloat16)

        @pl.when(seq > 0)
        def _():
            up.wait_recv()

        @pl.when(seq == 0)
        def _():
            lows[pl.ds(pad - rim, rim), :] = jnp.zeros((rim, 256), jnp.float32)

        @pl.when(seq < SEQ - 1)
        def _():
            down.wait_recv()

        @pl.when(seq == SEQ - 1)
        def _():
            highs[pl.ds(rows, rim), :] = jnp.zeros((rim, 256), jnp.float32)

        tile = 64
        for start in range(0, rows, tile):
            conv = (
                low_ext[layer % 2, pl.ds(pad - spread + start, tile), :]
                + pltpu.roll(middle[pl.ds(start, tile), :], 192, 1)
                + high_ext[layer % 2, pl.ds(spread + start, tile), :]
                + conv_bias[pl.ds(layer, 1), :]
            )
            hid[ch, pl.ds(start, tile), :] = gelu(conv).astype(jnp.bfloat16)

        first, second, third = spread_copies(hid, hid_send, hid_recv, layer)
        first.start()
        second.start()

        @pl.when(seq < SEQ - 1)
        def _():
            up.wait_send()

        @pl.when(seq > 0)
        def _():
            down.wait_send()

        slot(layer + 1, 1)
        first.wait_recv()
        third.start()
        slot(layer + 1, 2)
        second.wait_recv()
        third.wait_recv()
        mixed = streams[ch].astype(jnp.float32) + point_bias_ref[pl.ds(layer, 1), :]
        total = None
        for block in range(CHS):
            term = jnp.dot(
                hid[block, :, 0:192],
                point[block * 192 : (block + 1) * 192, :],
                preferred_element_type=jnp.float32,
            )
            total = term if total is None else total + term
        streams[ch] = (mixed + total).astype(jnp.bfloat16)
        for copy in (first, second, third):
            copy.wait_send()

    gather_stream(LAYERS)

    for start in range(0, heads.shape[2], 256):
        lanes = pl.ds(start, 256)
        logits = (
            jnp.dot(
                act[...],
                heads[:, :, start : start + 256].reshape(-1, 256),
                preferred_element_type=jnp.float32,
            )
            + head_bias[:, lanes]
        )
        cover = jnp.maximum(logits, 0.0) + jnp.log1p(jnp.exp(-jnp.abs(logits)))
        sums = None
        for _ in range(3):
            piece = cover.astype(jnp.bfloat16)
            term = jnp.dot(counts[...], piece, preferred_element_type=jnp.float32)
            sums = term if sums is None else sums + term
            cover = cover - piece.astype(jnp.float32)
        partial[:, :, lanes] = sums.reshape(SEQ, -1, 256)

    def sum_copy(step):
        target = (seq + step) % SEQ
        return pltpu.make_async_remote_copy(
            src_ref=partial.at[target],
            dst_ref=landed.at[step - 1],
            send_sem=sum_send.at[step - 1],
            recv_sem=sum_recv.at[step - 1],
            device_id=(target, ch),
            device_id_type=MESH,
        )

    for step in range(1, SEQ):
        sum_copy(step).start()
    for item in range(LAYERS + 1):
        for half in (0, 1):
            for way in (0, 1):
                for dist in range(1, reach(way, half) + 1):
                    ring_copy(item, half, dist, way).wait_send()
    result = partial[seq]
    for step in range(1, SEQ):
        sum_copy(step).wait_recv()
        result = result + landed[step - 1]
    out_ref[...] = jnp.log1p(result)[:, : out_ref.shape[1]]
    for step in range(1, SEQ):
        sum_copy(step).wait_send()


def local_kernel(
    stream,
    norm_gain,
    conv_weight,
    conv_bias,
    point_weight,
    point_bias,
    head_weight,
    head_bias,
    exon_start,
    exon_length,
    exon_transcript,
    transcript_slot,
):
    rows, width = stream.shape
    depth = conv_weight.shape[2]
    tracks = head_weight.shape[1]
    wide = -(-tracks // 256) * 256
    slots = transcript_slot.shape[0]
    vmem = pl.BlockSpec(memory_space=pltpu.VMEM)
    dma = pltpu.SemaphoreType.DMA
    return pl.pallas_call(
        tower_kernel,
        out_shape=jax.ShapeDtypeStruct((slots // SEQ, tracks), jnp.float32),
        in_specs=[vmem] * 12,
        out_specs=vmem,
        scratch_shapes=[
            pltpu.VMEM((LAYERS, SEQ, depth, 768), jnp.bfloat16),
            pltpu.VMEM((SEQ, depth, wide), jnp.bfloat16),
            pltpu.VMEM((CHS, rows, width), jnp.bfloat16),
            pltpu.VMEM((rows, CHS * width), jnp.bfloat16),
            pltpu.VMEM((2, rows + 128, 256), jnp.float32),
            pltpu.VMEM((2, rows + 128, 256), jnp.float32),
            pltpu.VMEM((rows, 256), jnp.float32),
            pltpu.VMEM((CHS, rows, 256), jnp.bfloat16),
            pltpu.VMEM((SEQ * HALF, width), jnp.bfloat16),
            pltpu.VMEM((SEQ, slots // SEQ, wide), jnp.float32),
            pltpu.VMEM((SEQ - 1, slots // SEQ, wide), jnp.float32),
            pltpu.VMEM((slots, rows), jnp.bfloat16),
            pltpu.VMEM((LAYERS, 256), jnp.float32),
            pltpu.VMEM((1, wide), jnp.float32),
            dma((2, LAYERS + 1, 2, 4)),
            dma((2, LAYERS + 1, 2, 4)),
            dma((LAYERS + 1, 3)),
            dma((LAYERS + 1, 3)),
            dma((LAYERS, 3)),
            dma((LAYERS, 3)),
            dma((2, LAYERS)),
            dma((2, LAYERS)),
            dma((SEQ - 1,)),
            dma((SEQ - 1,)),
        ],
        compiler_params=pltpu.CompilerParams(
            collective_id=0, has_side_effects=True, vmem_limit_bytes=56 * 2**20
        ),
        cost_estimate=pl.CostEstimate(
            flops=6_000_000_000, bytes_accessed=4_000_000, transcendentals=4_000_000
        ),
    )(
        stream,
        norm_gain,
        conv_weight,
        conv_bias,
        point_weight,
        point_bias,
        head_weight,
        head_bias[None, :],
        exon_start[None, :],
        exon_length[None, :],
        exon_transcript[None, :],
        transcript_slot[None, :],
    )


def local(*args):
    stream, conv_weight, point_weight = args[0], args[2], args[4]
    fits = (
        lax.axis_size("seq") == SEQ
        and lax.axis_size("ch") == CHS
        and stream.shape == (256, 384)
        and conv_weight.shape[2:] == (192, 192)
        and point_weight.shape[1:] == (HALF, 384)
        and args[11].shape[0] == 8 * SEQ
    )
    return local_kernel(*args) if fits else local_plain(*args)


def solution(mesh):
    placed = (
        P("seq", "ch"),
        P(),
        P(None, None, "seq", "ch"),
        P(None, "ch"),
        P(None, "seq", "ch"),
        P(None, "ch"),
        P("seq", "ch"),
        P("ch"),
        P(),
        P(),
        P(),
        P(),
    )
    return jax.shard_map(
        local, mesh=mesh, in_specs=placed, out_specs=P("seq", "ch"), check_vma=False
    )
```

```python
import jax
import jax.numpy as jnp
from jax import lax
from jax.experimental import pallas as pl
from jax.experimental.pallas import tpu as pltpu
from jax.sharding import PartitionSpec as P

LAYERS = 8


def padded(block, sides, width):
    for axis, dim in sides:
        count = lax.axis_size(axis)
        forward = [(i, i + 1) for i in range(count - 1)]
        backward = [(target, source) for source, target in forward]
        low = lax.ppermute(
            lax.slice_in_dim(block, block.shape[dim] - width, None, axis=dim), axis, forward
        )
        high = lax.ppermute(lax.slice_in_dim(block, 0, width, axis=dim), axis, backward)
        block = jnp.concatenate([low, block, high], axis=dim)
    return block


def rms_scaled(values, gain_row):
    wide = values.astype(jnp.float32)
    scale = lax.rsqrt(jnp.mean(wide * wide, axis=-1, keepdims=True) + 1e-06)
    return wide * scale * gain_row


def local_plain(
    stream,
    norm_gain,
    conv_weight,
    conv_bias,
    point_weight,
    point_bias,
    head_weight,
    head_bias,
    exon_start,
    exon_length,
    exon_transcript,
    transcript_slot,
):
    bin_rows = stream.shape[0]
    resid = stream
    for layer_idx in range(LAYERS):
        spread = 2**layer_idx
        rimmed = padded(resid, (("seq", 0),), spread)
        full_rows = lax.all_gather(rimmed, "ch", axis=1, tiled=True)
        act_rows = jax.nn.gelu(
            rms_scaled(full_rows, norm_gain[layer_idx]), approximate=False
        ).astype(jnp.bfloat16)
        tap_rows = jnp.stack(
            [
                act_rows[0:bin_rows],
                act_rows[spread : spread + bin_rows],
                act_rows[2 * spread : 2 * spread + bin_rows],
            ]
        )
        conv_sum = jnp.einsum(
            "kbc,kch->bh",
            tap_rows,
            lax.all_gather(conv_weight[layer_idx], "seq", axis=1, tiled=True),
            preferred_element_type=jnp.float32,
        )
        hidden = jax.nn.gelu(conv_sum + conv_bias[layer_idx], approximate=False).astype(
            jnp.bfloat16
        )
        hidden_all = lax.all_gather(hidden, "ch", axis=1, tiled=True)
        mixed = jnp.dot(
            hidden_all,
            lax.all_gather(point_weight[layer_idx], "seq", axis=0, tiled=True),
            preferred_element_type=jnp.float32,
        )
        resid = (resid.astype(jnp.float32) + mixed + point_bias[layer_idx]).astype(jnp.bfloat16)
    final_all = lax.all_gather(resid, "ch", axis=1, tiled=True)
    final_rows = rms_scaled(final_all, norm_gain[LAYERS]).astype(jnp.bfloat16)
    logits = jnp.dot(
        final_rows,
        lax.all_gather(head_weight, "seq", axis=0, tiled=True),
        preferred_element_type=jnp.float32,
    )
    coverage = jax.nn.softplus(logits + head_bias)
    seq_index = lax.axis_index("seq")
    bin_ids = seq_index * bin_rows + jnp.arange(bin_rows, dtype=jnp.int32)
    member = (
        (bin_ids[None, :] >= exon_start[:, None])
        & (bin_ids[None, :] < (exon_start + exon_length)[:, None])
    ).astype(jnp.bfloat16)
    owner_rows = transcript_slot[exon_transcript]
    select = (
        owner_rows[None, :] == jnp.arange(transcript_slot.shape[0], dtype=jnp.int32)[:, None]
    ).astype(jnp.bfloat16)
    counts = jnp.dot(select, member, preferred_element_type=jnp.float32)
    total = lax.psum_scatter(
        jnp.dot(counts, coverage, precision=lax.Precision.HIGHEST),
        "seq",
        scatter_dimension=0,
        tiled=True,
    )
    return jnp.log1p(total)


SEQ = 8
CHS = 4
HALF = 96
ITEMS = LAYERS + 2
MESH = pl.DeviceIdType.MESH


def gelu(values):
    return 0.5 * values * (1.0 + lax.erf(values * 0.7071067811865476))


def tower_kernel(
    x_ref,
    gain_ref,
    conv_ref,
    conv_bias_ref,
    point_ref,
    point_bias_ref,
    head_ref,
    head_bias_ref,
    start_ref,
    length_ref,
    owner_ref,
    slot_ref,
    out_ref,
    weights,
    heads,
    streams,
    act,
    low_ext,
    high_ext,
    middle,
    hid,
    point,
    partial,
    landed,
    counts,
    conv_bias,
    head_bias,
    ring_send,
    ring_recv,
    x_send,
    x_recv,
    hid_send,
    hid_recv,
    halo_send,
    halo_recv,
    sum_send,
    sum_recv,
):
    seq = lax.axis_index("seq")
    ch = lax.axis_index("ch")
    rows = x_ref.shape[0]
    odd = seq % 2
    place = (1 - odd) * (seq // 2) + odd * (SEQ - 1 - seq // 2)

    def at_place(spot):
        spot = (spot + 2 * SEQ) % SEQ
        upper = spot // (SEQ // 2)
        return (1 - upper) * 2 * spot + upper * (2 * (SEQ - 1 - spot) + 1)

    ring_to = (at_place(place + 1), at_place(place - 1))
    sibling = ch + 1 - 2 * (ch % 2)
    across = (ch + 2) % CHS
    diagonal = (sibling + 2) % CHS

    barrier = pltpu.get_barrier_semaphore()
    for step in range(1, SEQ):
        pl.semaphore_signal(
            barrier, inc=1, device_id=((seq + step) % SEQ, ch), device_id_type=MESH
        )
    for peer in (sibling, across):
        pl.semaphore_signal(barrier, inc=1, device_id=(seq, peer), device_id_type=MESH)

    def pack(item):
        if item < LAYERS:
            last = point_ref[item, :, 256:384]
            strip = jnp.concatenate([last[:, 0:64], last[:, 64:128]], axis=0)
            own = weights.at[item, seq]
            own[:, 0:640] = jnp.concatenate(
                [conv_ref[item, 0], conv_ref[item, 1], conv_ref[item, 2], strip], axis=1
            )
            own[0:HALF, 640:768] = point_ref[item, :, 0:128]
            own[HALF : 2 * HALF, 640:768] = point_ref[item, :, 128:256]
        else:
            depth, tracks = head_ref.shape
            span = heads.shape[3]
            first = (item - LAYERS) * span
            count = min(span, tracks - first)
            own = heads.at[item - LAYERS, seq]
            if count < span:
                own[:, count // 128 * 128 :] = jnp.zeros(
                    (depth, span - count // 128 * 128), jnp.bfloat16
                )
            own[:, 0:count] = head_ref[:, first : first + count]

    pack(0)
    streams[ch] = x_ref[...]
    pl.semaphore_wait(barrier, SEQ + 1)

    def reach(way, half):
        return 4 if way == half else 3

    def ring_copy(item, half, dist, way):
        origin = at_place(place - (dist - 1) if way == 0 else place + (dist - 1))
        part = pl.ds(half * HALF, HALF)
        if item < LAYERS:
            block = weights.at[item, origin, part]
        else:
            block = heads.at[item - LAYERS, origin, part]
        return pltpu.make_async_remote_copy(
            src_ref=block,
            dst_ref=block,
            send_sem=ring_send.at[way, item, half, dist - 1],
            recv_sem=ring_recv.at[way, item, half, dist - 1],
            device_id=(ring_to[way], ch),
            device_id_type=MESH,
        )

    def service(item, half, dist):
        for way in (0, 1):
            far = reach(way, half)
            if dist <= far:
                ring_copy(item, half, dist, way).wait_recv()
                if dist < far:
                    ring_copy(item, half, dist + 1, way).start()

    order = sorted((7 * item + 2 * number, item, number) for item in range(ITEMS) for number in range(7))
    steps = iter(order)

    def advance(count=1):
        for _, item, number in [next(steps) for _ in range(count)]:
            if number < 6:
                service(item, number % 2, number // 2 + 1)
            else:
                service(item, 0, 4)
                service(item, 1, 4)
            if number in (1, 2) and item + 1 < ITEMS:
                for way in (0, 1):
                    ring_copy(item + 1, number - 1, 1, way).start()

    for half in (0, 1):
        for way in (0, 1):
            ring_copy(0, half, 1, way).start()
    for item in range(1, ITEMS):
        pack(item)

    slots = slot_ref.shape[1]
    bins = seq * rows + lax.broadcasted_iota(jnp.int32, (rows, start_ref.shape[1]), 0)
    member = (bins >= start_ref[...]) & (bins < start_ref[...] + length_ref[...])
    names = lax.broadcasted_iota(jnp.int32, (slots, owner_ref.shape[1]), 0)
    owned = lax.dot_general(
        jnp.where(names == owner_ref[...], 1.0, 0.0).astype(jnp.bfloat16),
        jnp.where(member, 1.0, 0.0).astype(jnp.bfloat16),
        (((1,), (1,)), ((), ())),
        preferred_element_type=jnp.float32,
    )
    placed = lax.broadcasted_iota(jnp.int32, (slots, slots), 0) == slot_ref[...]
    counts[...] = jnp.dot(
        jnp.where(placed, 1.0, 0.0).astype(jnp.bfloat16),
        owned.astype(jnp.bfloat16),
        preferred_element_type=jnp.float32,
    ).astype(jnp.bfloat16)
    conv_bias[...] = jnp.zeros_like(conv_bias)
    conv_bias[:, 0 : conv_bias_ref.shape[1]] = conv_bias_ref[...]
    head_bias[...] = jnp.zeros_like(head_bias)
    head_bias[:, 0 : head_bias_ref.shape[1]] = head_bias_ref[...]

    def spread_copies(buffer, sends, recvs, turn):
        def copy(block, peer, number):
            return pltpu.make_async_remote_copy(
                src_ref=buffer.at[block],
                dst_ref=buffer.at[block],
                send_sem=sends.at[turn, number],
                recv_sem=recvs.at[turn, number],
                device_id=(seq, peer),
                device_id_type=MESH,
            )

        return copy(ch, across, 0), copy(ch, sibling, 1), copy(across, sibling, 2)

    def norm_rows(turn, first, count, finish):
        tile = 32

        @pl.loop(0, count // tile)
        def _(index):
            part = pl.ds(pl.multiple_of(first + index * tile, tile), tile)
            blocks = [streams[block, part, :].astype(jnp.float32) for block in range(CHS)]
            width = blocks[0].shape[1]
            squares = sum(jnp.sum(b * b, axis=1, keepdims=True) for b in blocks)
            scale = lax.rsqrt(squares / (width * CHS) + 1e-06)
            for block in range(CHS):
                lanes = pl.ds(block * width, width)
                normed = blocks[block] * scale * gain_ref[pl.ds(turn, 1), lanes]
                act[part, lanes] = finish(normed).astype(jnp.bfloat16)

    def gather_stream(turn):
        first, second, third = spread_copies(streams, x_send, x_recv, turn)
        finish = gelu if turn < LAYERS else (lambda normed: normed)
        first.start()
        second.start()
        advance()
        first.wait_recv()
        third.start()
        advance()
        second.wait_recv()
        third.wait_recv()
        norm_rows(turn, 0, rows // 2, finish)
        advance()
        norm_rows(turn, rows // 2, rows // 2, finish)
        for copy in (first, second, third):
            copy.wait_send()
        advance()

    advance(6)

    for layer in range(LAYERS):
        spread = 2**layer
        rim = max(8, spread)
        pad = low_ext.shape[1] - rows
        gather_stream(layer)
        lows, highs = low_ext.at[layer % 2], high_ext.at[layer % 2]

        both = jnp.dot(
            act[...],
            weights[layer, :, :, 0:384].reshape(-1, 384),
            preferred_element_type=jnp.float32,
        )
        lows[pl.ds(pad, rows), :] = both[:, 0:256]
        middle[...] = both[:, 128:384]
        highs[pl.ds(0, rows), :] = jnp.dot(
            act[...],
            weights[layer, :, :, 384:640].reshape(-1, 256),
            preferred_element_type=jnp.float32,
        )

        up = pltpu.make_async_remote_copy(
            src_ref=lows.at[pl.ds(pad + rows - rim, rim)],
            dst_ref=lows.at[pl.ds(pad - rim, rim)],
            send_sem=halo_send.at[0, layer],
            recv_sem=halo_recv.at[0, layer],
            device_id=((seq + 1) % SEQ, ch),
            device_id_type=MESH,
        )
        down = pltpu.make_async_remote_copy(
            src_ref=highs.at[pl.ds(0, rim)],
            dst_ref=highs.at[pl.ds(rows, rim)],
            send_sem=halo_send.at[1, layer],
            recv_sem=halo_recv.at[1, layer],
            device_id=((seq + SEQ - 1) % SEQ, ch),
            device_id_type=MESH,
        )

        @pl.when(seq < SEQ - 1)
        def _():
            up.start()

        @pl.when(seq > 0)
        def _():
            down.start()

        advance()

        for block in range(SEQ):
            here = pl.ds(block * HALF, HALF)
            point[here, 0:128] = weights[layer, block, 0:HALF, 640:768]
            point[here, 128:256] = weights[layer, block, HALF : 2 * HALF, 640:768]
            near = weights[layer, block, 0:HALF, 512:640].astype(jnp.float32)
            far = weights[layer, block, HALF : 2 * HALF, 512:640].astype(jnp.float32)
            lane = lax.broadcasted_iota(jnp.int32, near.shape, 1)
            point[here, 256:384] = jnp.where(
                lane < 64, pltpu.roll(near, 64, 1), far
            ).astype(jnp.bfloat16)

        @pl.when(seq > 0)
        def _():
            up.wait_recv()

        @pl.when(seq == 0)
        def _():
            lows[pl.ds(pad - rim, rim), :] = jnp.zeros((rim, 256), jnp.float32)

        @pl.when(seq < SEQ - 1)
        def _():
            down.wait_recv()

        @pl.when(seq == SEQ - 1)
        def _():
            highs[pl.ds(rows, rim), :] = jnp.zeros((rim, 256), jnp.float32)

        tile = 64
        for start in range(0, rows, tile):
            conv = (
                low_ext[layer % 2, pl.ds(pad - spread + start, tile), :]
                + pltpu.roll(middle[pl.ds(start, tile), :], 192, 1)
                + high_ext[layer % 2, pl.ds(spread + start, tile), :]
                + conv_bias[pl.ds(layer, 1), :]
            )
            hid[ch, pl.ds(start, tile), :] = gelu(conv).astype(jnp.bfloat16)

        first, second, third = spread_copies(hid, hid_send, hid_recv, layer)
        first.start()
        second.start()

        @pl.when(seq < SEQ - 1)
        def _():
            up.wait_send()

        @pl.when(seq > 0)
        def _():
            down.wait_send()

        advance()
        first.wait_recv()
        third.start()
        advance()
        second.wait_recv()
        third.wait_recv()
        mixed = streams[ch].astype(jnp.float32) + point_bias_ref[pl.ds(layer, 1), :]
        total = None
        for block in range(CHS):
            term = jnp.dot(
                hid[block, :, 0:192],
                point[block * 192 : (block + 1) * 192, :],
                preferred_element_type=jnp.float32,
            )
            total = term if total is None else total + term
        streams[ch] = (mixed + total).astype(jnp.bfloat16)
        for copy in (first, second, third):
            copy.wait_send()

    gather_stream(LAYERS)

    span = heads.shape[3]
    for start in range(0, 2 * span, 256):
        lanes = pl.ds(start, 256)
        if start <= span:
            advance(1 if start < span else 4 - span // 256)
        logits = (
            jnp.dot(
                act[...],
                heads[start // span, :, :, start % span : start % span + 256].reshape(-1, 256),
                preferred_element_type=jnp.float32,
            )
            + head_bias[:, lanes]
        )
        cover = jnp.maximum(logits, 0.0) + jnp.log1p(jnp.exp(-jnp.abs(logits)))
        sums = None
        for _ in range(3):
            piece = cover.astype(jnp.bfloat16)
            term = jnp.dot(counts[...], piece, preferred_element_type=jnp.float32)
            sums = term if sums is None else sums + term
            cover = cover - piece.astype(jnp.float32)
        partial[:, :, lanes] = sums.reshape(SEQ, -1, 256)

    def sum_copy(step):
        target = (seq + step) % SEQ
        return pltpu.make_async_remote_copy(
            src_ref=partial.at[target],
            dst_ref=landed.at[step - 1],
            send_sem=sum_send.at[step - 1],
            recv_sem=sum_recv.at[step - 1],
            device_id=(target, ch),
            device_id_type=MESH,
        )

    for step in range(1, SEQ):
        sum_copy(step).start()
    for item in range(ITEMS):
        for half in (0, 1):
            for way in (0, 1):
                for dist in range(1, reach(way, half) + 1):
                    ring_copy(item, half, dist, way).wait_send()
    result = partial[seq]
    for step in range(1, SEQ):
        sum_copy(step).wait_recv()
        result = result + landed[step - 1]
    out_ref[...] = jnp.log1p(result)[:, : out_ref.shape[1]]
    for step in range(1, SEQ):
        sum_copy(step).wait_send()


def local_kernel(
    stream,
    norm_gain,
    conv_weight,
    conv_bias,
    point_weight,
    point_bias,
    head_weight,
    head_bias,
    exon_start,
    exon_length,
    exon_transcript,
    transcript_slot,
):
    rows, width = stream.shape
    depth = conv_weight.shape[2]
    tracks = head_weight.shape[1]
    wide = -(-tracks // 256) * 256
    slots = transcript_slot.shape[0]
    vmem = pl.BlockSpec(memory_space=pltpu.VMEM)
    dma = pltpu.SemaphoreType.DMA
    return pl.pallas_call(
        tower_kernel,
        out_shape=jax.ShapeDtypeStruct((slots // SEQ, tracks), jnp.float32),
        in_specs=[vmem] * 12,
        out_specs=vmem,
        scratch_shapes=[
            pltpu.VMEM((LAYERS, SEQ, depth, 768), jnp.bfloat16),
            pltpu.VMEM((2, SEQ, depth, wide // 2), jnp.bfloat16),
            pltpu.VMEM((CHS, rows, width), jnp.bfloat16),
            pltpu.VMEM((rows, CHS * width), jnp.bfloat16),
            pltpu.VMEM((2, rows + 128, 256), jnp.float32),
            pltpu.VMEM((2, rows + 128, 256), jnp.float32),
            pltpu.VMEM((rows, 256), jnp.float32),
            pltpu.VMEM((CHS, rows, 256), jnp.bfloat16),
            pltpu.VMEM((SEQ * HALF, width), jnp.bfloat16),
            pltpu.VMEM((SEQ, slots // SEQ, wide), jnp.float32),
            pltpu.VMEM((SEQ - 1, slots // SEQ, wide), jnp.float32),
            pltpu.VMEM((slots, rows), jnp.bfloat16),
            pltpu.VMEM((LAYERS, 256), jnp.float32),
            pltpu.VMEM((1, wide), jnp.float32),
            dma((2, ITEMS, 2, 4)),
            dma((2, ITEMS, 2, 4)),
            dma((LAYERS + 1, 3)),
            dma((LAYERS + 1, 3)),
            dma((LAYERS, 3)),
            dma((LAYERS, 3)),
            dma((2, LAYERS)),
            dma((2, LAYERS)),
            dma((SEQ - 1,)),
            dma((SEQ - 1,)),
        ],
        compiler_params=pltpu.CompilerParams(
            collective_id=0, has_side_effects=True, vmem_limit_bytes=56 * 2**20
        ),
        cost_estimate=pl.CostEstimate(
            flops=6_000_000_000, bytes_accessed=4_000_000, transcendentals=4_000_000
        ),
    )(
        stream,
        norm_gain,
        conv_weight,
        conv_bias,
        point_weight,
        point_bias,
        head_weight,
        head_bias[None, :],
        exon_start[None, :],
        exon_length[None, :],
        exon_transcript[None, :],
        transcript_slot[None, :],
    )


def local(*args):
    stream, conv_weight, point_weight = args[0], args[2], args[4]
    fits = (
        lax.axis_size("seq") == SEQ
        and lax.axis_size("ch") == CHS
        and stream.shape == (256, 384)
        and conv_weight.shape[2:] == (192, 192)
        and point_weight.shape[1:] == (HALF, 384)
        and args[11].shape[0] == 8 * SEQ
    )
    return local_kernel(*args) if fits else local_plain(*args)


def solution(mesh):
    placed = (
        P("seq", "ch"),
        P(),
        P(None, None, "seq", "ch"),
        P(None, "ch"),
        P(None, "seq", "ch"),
        P(None, "ch"),
        P("seq", "ch"),
        P("ch"),
        P(),
        P(),
        P(),
        P(),
    )
    return jax.shard_map(
        local, mesh=mesh, in_specs=placed, out_specs=P("seq", "ch"), check_vma=False
    )
```
